32 devices in a mesh: section: 4 (over z), expert: 4 (over y, x), dp: 2 (over core).
Axes of the slice: x: 2, y: 2, z: 4, core: 2. Of those that a mesh axis runs over, the one named last changes fastest.
Arguments:
- tokens_fwd: bfloat16 [2048, 2560], P(('section', 'expert', 'dp')), may hold values from -6 to 6
- route_fwd: int32 [2048], P(('section', 'expert', 'dp')), may hold values from 0 to 1, as said below
- gate_fwd: float32 [2048], P(('section', 'expert', 'dp')), may hold values from 0.2 to 1
- grad_out: bfloat16 [2048, 2560], P(('section', 'expert', 'dp')), may hold values from -3 to 3
- route_bwd: int32 [2048], P(('section', 'expert', 'dp')), may hold values from 0 to 1, as said below
- gate_bwd: float32 [2048], P(('section', 'expert', 'dp')), may hold values from 0.2 to 1
- saved_pre: bfloat16 [4, 2, 128, 1536], P('section', 'dp', None, 'expert'), may hold values from -6 to 6
- w_up: bfloat16 [4, 2560, 1536], P('section', None, 'expert'), may hold values from -0.125 to 0.125
- w_down: bfloat16 [4, 1536, 2560], P('section', 'expert'), may hold values from -0.21875 to 0.21875
- basis_q: float32 [2560, 64], replicated, may hold values from -6 to 6
Outputs:
- expert_out: bfloat16 [2048, 2560], P(('section', 'expert', 'dp'))
- grad_in: bfloat16 [2048, 2560], P(('section', 'expert', 'dp'))
- factor_p: float32 [4, 1536, 64], P('section', 'expert')
- factor_q: bfloat16 [4, 4, 2560, 64], P('section', 'expert')
The draws below stay inside these ranges and needn't reach their ends.
Inputs may be any that keep to these rules, and one draw needn't show every extreme that they name: `route_fwd`: each device's 64 tokens name each of the 2 live experts exactly 32 times. `route_bwd`: each device's 64 tokens name each of the 2 live experts exactly 32 times.
All inputs are finite; a program needn't handle non-finite values.
Results may differ from the reference program's by a relative error of at most 0.0065.
Values may be sent and summed in bfloat16 or wider, within the bound.
A program may use at most 64 MiB of HBM per device.

```python
import math
import jax
import jax.numpy as jnp
from jax import lax

D = 2560
HIDDEN_SIZE = 768
RANK = 64
TOK_DEV = 64
EXPERTS = 2
HS = 384
CAP = 32
SLOTS = 128
UNITS = 1536
ROWS = 2048
N_SECTION = 4
N_EXPERT = 4
N_DP = 2


def balanced_routes(key):
    block_count = ROWS // TOK_DEV
    pattern = jnp.repeat(jnp.arange(EXPERTS, dtype=jnp.int32), CAP)
    keys = jax.random.split(key, block_count)
    shuffled = jax.vmap(lambda single: jax.random.permutation(single, pattern))(keys)
    return shuffled.reshape(ROWS).astype(jnp.int32)


def draw_route_fwd(key, part):
    return balanced_routes(jax.random.fold_in(key, 101))


def draw_route_bwd(key, part):
    return balanced_routes(jax.random.fold_in(key, 202))


def block_levels(own_key, shape, shards, low, high):
    gain = 1.0
    for dim, blocks in shards:
        steps = jax.random.uniform(jax.random.fold_in(jax.random.fold_in(own_key, 6), dim), (blocks,), jnp.float32, low / len(shards), high / len(shards))
        gain = gain * jnp.repeat(jnp.exp(steps), shape[dim] // blocks).reshape((-1,) + (1,) * (len(shape) - 1 - dim))
    return gain


def scatter_about(rng, shape, scale, most, pieces=(), kind=jnp.bfloat16):
    entries = scale * jax.random.normal(rng, shape, jnp.float32)
    if pieces:
        entries = entries * block_levels(rng, shape, pieces, -0.22, 0.18)
    return jnp.clip(entries, -most, most).astype(kind)


def setup_inputs(seed: int = 0) -> dict:
    arg_keys = jax.random.split(jax.random.key(seed), 11)
    return {
        "tokens_fwd": scatter_about(arg_keys[0], (ROWS, D), 1.0, 6.0, ((0, 32),)),
        "route_fwd": draw_route_fwd(jax.random.fold_in(arg_keys[10], 71), 0),
        "gate_fwd": jnp.clip(jnp.exp(math.log(1.0) - 1.609438 * jax.random.uniform(arg_keys[2], (ROWS,), jnp.float32) ** block_levels(arg_keys[2], (ROWS,), ((0, 32),), -0.2, 0.2)), 0.2, 1.0),
        "grad_out": scatter_about(arg_keys[3], (ROWS, D), 0.5, 3.0, ((0, 32),)),
        "route_bwd": draw_route_bwd(jax.random.fold_in(arg_keys[10], 71), 0),
        "gate_bwd": jnp.clip(jnp.exp(math.log(1.0) - 1.609438 * jax.random.uniform(arg_keys[5], (ROWS,), jnp.float32) ** block_levels(arg_keys[5], (ROWS,), ((0, 32),), -0.2, 0.2)), 0.2, 1.0),
        "saved_pre": scatter_about(arg_keys[6], (N_SECTION, N_DP, SLOTS, UNITS), 1.0, 6.0, ((0, 4), (1, 2), (3, 4))),
        "w_up": scatter_about(arg_keys[7], (N_SECTION, D, UNITS), D ** -0.5, 0.125, ((0, 4), (2, 4))),
        "w_down": scatter_about(arg_keys[8], (N_SECTION, UNITS, D), HIDDEN_SIZE ** -0.5, 0.21875, ((0, 4), (1, 4))),
        "basis_q": scatter_about(arg_keys[9], (D, RANK), 1.0, 6.0, (), jnp.float32),
    }


highest = lax.Precision.HIGHEST

def orthonormal(matrix):
    column_count = matrix.shape[1]

    def place_column(position, result):
        column = lax.dynamic_slice_in_dim(matrix, position, 1, 1)
        earlier = (jnp.arange(column_count, dtype=jnp.int32) < position).astype(matrix.dtype)[:, None]
        for repeat in range(2):
            project = jnp.dot(result.T, column, precision=highest) * earlier
            column = column - jnp.dot(result, project, precision=highest)
        column = column * lax.rsqrt(jnp.sum(column * column) + 1e-06)
        return lax.dynamic_update_slice_in_dim(result, column, position, 1)
    return lax.fori_loop(0, column_count, place_column, jnp.zeros_like(matrix))

def contract_last(left, right):
    return lax.dot_general(left, right, (((1,), (1,)), ((), ())), preferred_element_type=jnp.float32)

def group_slots(token_rows, routing):
    slot_order = jnp.argsort(routing, axis=1, stable=True).astype(jnp.int32)
    picked = jax.vmap(lambda rows_one, order_one: rows_one[order_one])(token_rows, slot_order)
    return (picked.reshape(N_EXPERT, EXPERTS, CAP, D), slot_order)

def combine_parts(parts, slot_order):
    parts = parts.reshape(EXPERTS, 2, N_EXPERT, CAP, D).astype(jnp.float32)
    mixed = (parts[:, 0] + parts[:, 1]).astype(jnp.bfloat16)
    mixed = jnp.transpose(mixed, (1, 0, 2, 3)).reshape(N_EXPERT, TOK_DEV, D)
    token_slot = jnp.argsort(slot_order, axis=1).astype(jnp.int32)
    return jax.vmap(lambda rows_one, order_one: rows_one[order_one])(mixed, token_slot)

def device_weights(up_section, down_section, device):
    up_cols = lax.dynamic_slice_in_dim(up_section, device * HS, HS, 1)
    down_rows = lax.dynamic_slice_in_dim(down_section, device * HS, HS, 0)
    return (up_cols, down_rows)

def forward_group(token_rows, routing, gating, up_section, down_section):
    picked, slot_order = group_slots(token_rows, routing)

    def device_part(device):
        inputs = lax.dynamic_index_in_dim(picked, device // 2, 1, keepdims=False).reshape(SLOTS, D)
        up_cols, down_rows = device_weights(up_section, down_section, device)
        hidden = jax.nn.silu(jnp.dot(inputs, up_cols, preferred_element_type=jnp.float32)).astype(jnp.bfloat16)
        return jnp.dot(hidden, down_rows, preferred_element_type=jnp.float32).astype(jnp.bfloat16)
    parts = lax.map(device_part, jnp.arange(N_EXPERT, dtype=jnp.int32))
    mixed = combine_parts(parts, slot_order)
    return (gating[:, :, None] * mixed.astype(jnp.float32)).astype(jnp.bfloat16)

def device_backward(picked, pre_group, up_section, down_section, device):
    grad_rows = lax.dynamic_index_in_dim(picked, device // 2, 1, keepdims=False).reshape(SLOTS, D)
    up_cols, down_rows = device_weights(up_section, down_section, device)
    preact = lax.dynamic_slice_in_dim(pre_group, device * HS, HS, 1).astype(jnp.float32)
    sigmoid_pre = jax.nn.sigmoid(preact)
    hidden_bwd = (preact * sigmoid_pre).astype(jnp.bfloat16)
    slope_term = sigmoid_pre * (1.0 + preact * (1.0 - sigmoid_pre))
    pre_grad = (contract_last(grad_rows, down_rows) * slope_term).astype(jnp.bfloat16)
    input_part = contract_last(pre_grad, up_cols).astype(jnp.bfloat16)
    weight_grad = lax.dot_general(hidden_bwd, grad_rows, (((0,), (0,)), ((), ())), preferred_element_type=jnp.float32)
    return (input_part, weight_grad)

def backward_group(token_rows, routing, pre_group, up_section, down_section, basis_q):
    picked, slot_order = group_slots(token_rows, routing)

    def device_part(device):
        input_part, weight_grad = device_backward(picked, pre_group, up_section, down_section, device)
        return (input_part, jnp.dot(weight_grad, basis_q, precision=highest))
    parts, left_terms = lax.map(device_part, jnp.arange(N_EXPERT, dtype=jnp.int32))
    return (combine_parts(parts, slot_order), left_terms)

def right_group(token_rows, routing, pre_group, up_section, down_section, left_section):
    picked, slot_order = group_slots(token_rows, routing)

    def device_part(device):
        input_part, weight_grad = device_backward(picked, pre_group, up_section, down_section, device)
        left_one = lax.dynamic_index_in_dim(left_section, device, 0, keepdims=False)
        return lax.dot_general(weight_grad, left_one, (((0,), (0,)), ((), ())), precision=highest, preferred_element_type=jnp.float32)
    return lax.map(device_part, jnp.arange(N_EXPERT, dtype=jnp.int32))

def reference(tokens_fwd, route_fwd, gate_fwd, grad_out, route_bwd, gate_bwd, saved_pre, w_up, w_down, basis_q):
    grid_shape = (N_SECTION, N_EXPERT, N_DP, TOK_DEV, D)
    token_grid = tokens_fwd.reshape(grid_shape)
    scaled = (gate_bwd[:, None] * grad_out.astype(jnp.float32)).astype(jnp.bfloat16).reshape(grid_shape)
    routing_fwd = route_fwd.reshape(grid_shape[:4])
    routing_bwd = route_bwd.reshape(grid_shape[:4])
    gating_fwd = gate_fwd.reshape(grid_shape[:4])

    def first_pass(section_index):
        up_section = w_up[section_index]
        down_section = w_down[section_index]
        outs_fwd = []
        outs_bwd = []
        left_list = []
        for replica in range(N_DP):
            outs_fwd.append(forward_group(token_grid[section_index, :, replica], routing_fwd[section_index, :, replica], gating_fwd[section_index, :, replica], up_section, down_section))
            grad_rows, left_terms = backward_group(scaled[section_index, :, replica], routing_bwd[section_index, :, replica], saved_pre[section_index, replica], up_section, down_section, basis_q)
            outs_bwd.append(grad_rows)
            left_list.append(left_terms)
        return (jnp.stack(outs_fwd, 1), jnp.stack(outs_bwd, 1), jnp.stack(left_list, 0))
    expert_out, grad_in, left_terms = lax.map(first_pass, jnp.arange(N_SECTION, dtype=jnp.int32))
    left_pair = lax.optimization_barrier(jnp.sum(left_terms + left_terms[::-1], axis=1))
    left_factor = jax.vmap(jax.vmap(orthonormal))(left_pair)

    def second_pass(section_index):
        up_section = w_up[section_index]
        down_section = w_down[section_index]
        total = jnp.zeros((N_EXPERT, D, RANK), jnp.float32)
        for replica in range(N_DP):
            total = total + right_group(scaled[section_index, :, replica], routing_bwd[section_index, :, replica], saved_pre[section_index, replica], up_section, down_section, left_factor[section_index])
        return total
    right_terms = lax.map(second_pass, jnp.arange(N_SECTION, dtype=jnp.int32))
    factor_q = (right_terms + right_terms[::-1]).astype(jnp.bfloat16)
    factor_p = left_factor.reshape(N_SECTION, N_EXPERT * HS, RANK)
    return (expert_out.reshape(ROWS, D), grad_in.reshape(ROWS, D), factor_p, factor_q)
```

```python
import functools

import jax
import jax.numpy as jnp
from jax import lax
from jax.experimental import pallas as pl
from jax.experimental.pallas import tpu as pltpu
from jax.sharding import PartitionSpec as P

highest = lax.Precision.HIGHEST
MESH = pl.DeviceIdType.MESH


def from_partner(value, axis, apart):
    mask = 2**apart
    pairs = [(source, source ^ mask) for source in range(lax.axis_size(axis))]
    return lax.ppermute(value, axis, pairs)


def orthonormal(matrix):
    column_count = matrix.shape[1]

    def place_column(position, result):
        column = lax.dynamic_slice_in_dim(matrix, position, 1, 1)
        earlier = (jnp.arange(column_count, dtype=jnp.int32) < position).astype(matrix.dtype)[
            :, None
        ]
        for repeat in range(2):
            project = jnp.dot(result.T, column, precision=highest) * earlier
            column = column - jnp.dot(result, project, precision=highest)
        column = column * lax.rsqrt(jnp.sum(column * column) + 1e-06)
        return lax.dynamic_update_slice_in_dim(result, column, position, 1)

    return lax.fori_loop(0, column_count, place_column, jnp.zeros_like(matrix))


def contract_last(left, right):
    return lax.dot_general(
        left, right, (((1,), (1,)), ((), ())), preferred_element_type=jnp.float32
    )


def spread_rows(picked):
    device_count = lax.axis_size("expert")
    experts_live = picked.shape[0]
    capacity = picked.shape[1]
    features = picked.shape[2]
    return jnp.broadcast_to(picked[:, None], (experts_live, 2, capacity, features)).reshape(
        device_count, capacity, features
    )


def send_rows(first_picked, second_picked):
    first_out = spread_rows(first_picked)
    second_out = spread_rows(second_picked)
    first_arrived, second_arrived = [
        lax.all_to_all(element, "expert", split_axis=0, concat_axis=0, tiled=True)
        for element in (first_out, second_out)
    ]
    features = first_arrived.shape[2]
    return (first_arrived.reshape(-1, features), second_arrived.reshape(-1, features))


def collect_rows(returned, experts_live):
    features = returned.shape[2]
    capacity = returned.shape[1]
    summed = returned.reshape(experts_live, 2, capacity, features).astype(jnp.float32)
    return (summed[:, 0] + summed[:, 1]).astype(jnp.bfloat16).reshape(-1, features)


def send_back(first_partial, second_partial, experts_live):
    device_count = lax.axis_size("expert")
    features = first_partial.shape[1]
    capacity = first_partial.shape[0] // device_count
    first_out = first_partial.reshape(device_count, capacity, features).astype(jnp.bfloat16)
    second_out = second_partial.reshape(device_count, capacity, features).astype(jnp.bfloat16)
    first_returned, second_returned = [
        lax.all_to_all(element, "expert", split_axis=0, concat_axis=0, tiled=True)
        for element in (first_out, second_out)
    ]
    return (collect_rows(first_returned, experts_live), collect_rows(second_returned, experts_live))


def pair_total(local_term):
    mirrored = local_term
    for bit_level in range(lax.axis_size("section").bit_length() - 1):
        mirrored = from_partner(mirrored, "section", bit_level)
    return lax.psum(local_term + mirrored, "dp")


def body(
    tokens_fwd, route_fwd, gate_fwd, grad_out, route_bwd, gate_bwd, saved_pre, w_up, w_down, basis_q
):
    device_count = lax.axis_size("expert")
    experts_live = device_count // 2
    token_count = tokens_fwd.shape[0]
    features = tokens_fwd.shape[1]
    capacity = token_count // experts_live
    up_cols = w_up[0]
    down_rows = w_down[0]
    order_fwd = jnp.argsort(route_fwd, stable=True)
    inverse_fwd = jnp.argsort(order_fwd)
    scaled = (gate_bwd[:, None] * grad_out.astype(jnp.float32)).astype(jnp.bfloat16)
    order_bwd = jnp.argsort(route_bwd, stable=True)
    inverse_bwd = jnp.argsort(order_bwd)
    inputs, grad_rows = send_rows(
        tokens_fwd[order_fwd].reshape(experts_live, capacity, features),
        scaled[order_bwd].reshape(experts_live, capacity, features),
    )
    hidden = jax.nn.silu(jnp.dot(inputs, up_cols, preferred_element_type=jnp.float32)).astype(
        jnp.bfloat16
    )
    partial_value = jnp.dot(hidden, down_rows, preferred_element_type=jnp.float32)
    preact = saved_pre[0, 0].astype(jnp.float32)
    sigmoid_pre = jax.nn.sigmoid(preact)
    hidden_bwd = (preact * sigmoid_pre).astype(jnp.bfloat16)
    slope_term = sigmoid_pre * (1.0 + preact * (1.0 - sigmoid_pre))
    pre_grad = (contract_last(grad_rows, down_rows) * slope_term).astype(jnp.bfloat16)
    input_part = contract_last(pre_grad, up_cols)
    mixed_sorted, grad_sorted = send_back(partial_value, input_part, experts_live)
    expert_out = (gate_fwd[:, None] * mixed_sorted[inverse_fwd].astype(jnp.float32)).astype(
        jnp.bfloat16
    )
    grad_in = grad_sorted[inverse_bwd]
    weight_grad = lax.dot_general(
        hidden_bwd, grad_rows, (((0,), (0,)), ((), ())), preferred_element_type=jnp.float32
    )
    left_term = jnp.dot(weight_grad, basis_q, precision=highest)
    left_factor = orthonormal(pair_total(left_term))
    right_term = lax.dot_general(
        weight_grad,
        left_factor,
        (((0,), (0,)), ((), ())),
        precision=highest,
        preferred_element_type=jnp.float32,
    )
    right_factor = pair_total(right_term).astype(jnp.bfloat16)
    return (expert_out, grad_in, left_factor[None], right_factor[None, None])


def slot_matrix(route_row, capacity):
    count = route_row.shape[1]
    first = lax.broadcasted_iota(jnp.int32, (count, count), 0)
    second = lax.broadcasted_iota(jnp.int32, (count, count), 1)
    across = jnp.broadcast_to(route_row.astype(jnp.float32), (count, count))
    down = jnp.sum(jnp.where(first == second, across, 0.0), axis=1, keepdims=True)
    ahead = jnp.where((down == across) & (first < second), 1.0, 0.0)
    slot = across * capacity + jnp.sum(ahead, axis=0, keepdims=True)
    return jnp.where(slot == first.astype(jnp.float32), 1.0, 0.0).astype(jnp.bfloat16)


def as_column(row):
    count = row.shape[1]
    first = lax.broadcasted_iota(jnp.int32, (count, count), 0)
    second = lax.broadcasted_iota(jnp.int32, (count, count), 1)
    return jnp.sum(jnp.where(first == second, row, 0.0), axis=1, keepdims=True)


def halves(value):
    high = value.astype(jnp.bfloat16)
    return high, (value - high.astype(jnp.float32)).astype(jnp.bfloat16)


def dot32(left, right, dims=((1,), (0,))):
    return lax.dot_general(left, right, (dims, ((), ())), preferred_element_type=jnp.float32)


def fused_kernel(
    sizes,
    tok_hbm, rf_ref, gf_ref, go_hbm, rb_ref, gb_ref, pre_hbm, up_hbm, down_hbm, basis_hbm,
    out_ref, gin_ref, p_ref, q_ref,
    tok_ref, go_ref, pre_ref, up, down, basis, sendz, sendx, zbuf, xbuf, partb, partf, retb, retf,
    lown, lpeer, lsum, lpart, amat, umat, rown, rpeer, rsum, zout, zin, qbuf,
    local_sem, zs, zr, xs, xr, bs, br, fs, fr, ps, pr,
):
    n, n_sec, cap = sizes
    live = n // 2
    me = lax.axis_index("expert")
    core = lax.axis_index("dp")
    sibling = {"dp": 1 - core}
    mirror = {"section": n_sec - 1 - lax.axis_index("section")}

    loads = [
        pltpu.make_async_copy(source, target, local_sem.at[i])
        for i, (source, target) in enumerate(
            (
                (go_hbm, go_ref), (tok_hbm, tok_ref), (pre_hbm, pre_ref),
                (basis_hbm, basis), (down_hbm, down), (up_hbm, up),
            )
        )
    ]
    for load in loads:
        load.start()

    barrier = pltpu.get_barrier_semaphore()
    for shift in range(1, n):
        pl.semaphore_signal(
            barrier, inc=1, device_id={"expert": lax.rem(me + shift, n)}, device_id_type=MESH
        )
    pl.semaphore_signal(barrier, inc=1, device_id=sibling, device_id_type=MESH)
    pl.semaphore_signal(barrier, inc=1, device_id=mirror, device_id_type=MESH)

    def rows_of(index):
        return pl.ds(pl.multiple_of(index * cap, cap), cap)

    def remote(source, target, send, recv, device):
        return pltpu.make_async_remote_copy(
            src_ref=source, dst_ref=target, send_sem=send, recv_sem=recv,
            device_id=device, device_id_type=MESH,
        )

    def dispatch(source, target, send, recv):
        copies = []
        for shift in range(1, n):
            to = lax.rem(me + shift, n)
            copies.append(
                remote(source.at[rows_of(to // 2)], target.at[rows_of(me)],
                       send.at[shift], recv.at[shift], {"expert": to})
            )
        for copy in copies:
            copy.start()
        target[rows_of(me)] = source[rows_of(me // 2)]
        return copies

    def send_back(source, target, send, recv):
        copies = []
        for shift in range(1, n):
            to = lax.rem(me + shift, n)
            copies.append(
                remote(source.at[rows_of(to)], target.at[rows_of(me)],
                       send.at[shift], recv.at[shift], {"expert": to})
            )
        for copy in copies:
            copy.start()
        target[rows_of(me)] = source[rows_of(me)]
        return copies

    def combine(returned):
        sums = [
            (
                returned[2 * e * cap : (2 * e + 1) * cap].astype(jnp.float32)
                + returned[(2 * e + 1) * cap : (2 * e + 2) * cap].astype(jnp.float32)
            ).astype(jnp.bfloat16)
            for e in range(live)
        ]
        return jnp.concatenate(sums, axis=0)

    place_bwd = slot_matrix(rb_ref[...], cap)
    loads[0].wait()
    scaled = (as_column(gb_ref[...]) * go_ref[...].astype(jnp.float32)).astype(jnp.bfloat16)
    sendz[...] = dot32(place_bwd, scaled).astype(jnp.bfloat16)
    pl.semaphore_wait(barrier, n + 1)
    z_copies = dispatch(sendz, zbuf, zs, zr)
    place_fwd = slot_matrix(rf_ref[...], cap)
    loads[1].wait()
    sendx[...] = dot32(place_fwd, tok_ref[...]).astype(jnp.bfloat16)
    x_copies = dispatch(sendx, xbuf, xs, xr)

    loads[2].wait()
    preact = pre_ref[...].astype(jnp.float32)
    sigmoid = jax.nn.sigmoid(preact)
    hidden_bwd = (preact * sigmoid).astype(jnp.bfloat16)
    slope = sigmoid * (1.0 + preact * (1.0 - sigmoid))

    loads[3].wait()
    basis_high, basis_low = halves(basis[...])
    for copy in z_copies:
        copy.wait()
    nt = ((1,), (1,))
    zb_high, zb_low = halves(dot32(basis_high, zbuf[...], nt) + dot32(basis_low, zbuf[...], nt))
    lown[...] = dot32(zb_high, hidden_bwd) + dot32(zb_low, hidden_bwd)
    left_dp = remote(lown, lpeer, ps.at[0], pr.at[0], sibling)
    left_dp.start()

    loads[4].wait()
    pre_grad = (dot32(zbuf[...], down[...], ((1,), (1,))) * slope).astype(jnp.bfloat16)
    left_dp.wait()
    lsum[...] = lown[...] + lpeer[...]
    left_z = remote(lsum, lpart, ps.at[1], pr.at[1], mirror)
    left_z.start()
    loads[5].wait()
    partb[...] = dot32(pre_grad, up[...], ((1,), (1,))).astype(jnp.bfloat16)
    b_copies = send_back(partb, retb, bs, br)

    for copy in x_copies:
        copy.wait()
    value = dot32(xbuf[...], up[...])
    hidden = (value * jax.nn.sigmoid(value)).astype(jnp.bfloat16)
    partf[...] = dot32(hidden, down[...]).astype(jnp.bfloat16)
    f_copies = send_back(partf, retf, fs, fr)

    left_z.wait()
    amat[...] = lsum[...] + lpart[...]
    umat[...] = jnp.zeros_like(umat)
    rank = amat.shape[0]

    def place(k, v):
        earlier = umat[...]
        follow = amat[pl.ds(lax.rem(k + 1, rank), 1), :]
        again = jnp.sum(earlier * v, axis=1, keepdims=True)
        ahead = jnp.sum(earlier * follow, axis=1, keepdims=True)
        v = v - jnp.sum(earlier * again, axis=0, keepdims=True)
        follow_left = follow - jnp.sum(earlier * ahead, axis=0, keepdims=True)
        square = jnp.sum(v * v, axis=1, keepdims=True)
        share = jnp.sum(v * follow, axis=1, keepdims=True)
        inverse = lax.rsqrt(square + 1e-06)
        unit = v * inverse
        umat[pl.ds(k, 1), :] = unit
        return follow_left - unit * (share * inverse)

    lax.fori_loop(0, rank, place, amat[pl.ds(0, 1), :])
    p_ref[...] = umat[...]

    u_high, u_low = halves(umat[...])
    hp_high, hp_low = halves(dot32(u_high, hidden_bwd, nt) + dot32(u_low, hidden_bwd, nt))
    rown[...] = dot32(hp_high, zbuf[...]) + dot32(hp_low, zbuf[...])
    half = rank // 2
    mine = pl.ds(pl.multiple_of(core * half, half), half)
    other = pl.ds(pl.multiple_of((1 - core) * half, half), half)
    right_dp = remote(rown.at[other], rpeer, ps.at[2], pr.at[2], sibling)
    right_dp.start()
    for copy in b_copies:
        copy.wait()
    gin_ref[...] = dot32(place_bwd, combine(retb), ((0,), (0,))).astype(jnp.bfloat16)
    right_dp.wait()
    rsum[...] = rown[mine] + rpeer[...]
    zout[...] = rsum[...].astype(jnp.bfloat16)
    right_z = remote(zout, zin, ps.at[3], pr.at[3], mirror)
    right_z.start()
    for copy in f_copies:
        copy.wait()
    mixed = dot32(place_fwd, combine(retf), ((0,), (0,)))
    out_ref[...] = (as_column(gf_ref[...]) * mixed).astype(jnp.bfloat16)
    right_z.wait()
    qbuf[mine] = (rsum[...] + zin[...].astype(jnp.float32)).astype(jnp.bfloat16)
    share_q = remote(qbuf.at[mine], qbuf.at[mine], ps.at[4], pr.at[4], sibling)
    share_q.start()
    share_q.wait()
    q_ref[...] = qbuf[...]


def fused_body(
    tokens_fwd, route_fwd, gate_fwd, grad_out, route_bwd, gate_bwd, saved_pre, w_up, w_down, basis_q
):
    n, n_sec = lax.axis_size("expert"), lax.axis_size("section")
    count, features = tokens_fwd.shape
    cap = count // (n // 2)
    slots, units = saved_pre.shape[2:]
    rank = basis_q.shape[1]
    bf, f32 = jnp.bfloat16, jnp.float32
    vmem = pl.BlockSpec(memory_space=pltpu.VMEM)
    hbm = pl.BlockSpec(memory_space=pl.ANY)
    wide = [pltpu.VMEM((slots, features), bf)]
    square = [pltpu.VMEM((rank, units), f32)]
    half = (rank // 2, features)
    expert_out, grad_in, left, right = pl.pallas_call(
        functools.partial(fused_kernel, (n, n_sec, cap)),
        out_shape=(
            jax.ShapeDtypeStruct((count, features), bf),
            jax.ShapeDtypeStruct((count, features), bf),
            jax.ShapeDtypeStruct((rank, units), f32),
            jax.ShapeDtypeStruct((rank, features), bf),
        ),
        in_specs=[hbm, vmem, vmem, hbm, vmem, vmem, hbm, hbm, hbm, hbm],
        out_specs=(vmem,) * 4,
        scratch_shapes=[
            pltpu.VMEM((count, features), bf),
            pltpu.VMEM((count, features), bf),
            pltpu.VMEM((slots, units), bf),
            pltpu.VMEM((features, units), bf),
            pltpu.VMEM((units, features), bf),
            pltpu.VMEM((rank, features), f32),
            pltpu.VMEM((count, features), bf),
            pltpu.VMEM((count, features), bf),
        ]
        + wide * 4
        + [pltpu.VMEM((n * cap, features), bf)] * 2
        + square * 6
        + [
            pltpu.VMEM((rank, features), f32),
            pltpu.VMEM(half, f32),
            pltpu.VMEM(half, f32),
            pltpu.VMEM(half, bf),
            pltpu.VMEM(half, bf),
            pltpu.VMEM((rank, features), bf),
            pltpu.SemaphoreType.DMA((6,)),
        ]
        + [pltpu.SemaphoreType.DMA((n,))] * 8
        + [pltpu.SemaphoreType.DMA((5,))] * 2,
        compiler_params=pltpu.CompilerParams(
            collective_id=0, has_side_effects=True, vmem_limit_bytes=63 * 2**20
        ),
    )(
        tokens_fwd, route_fwd[None], gate_fwd[None], grad_out, route_bwd[None], gate_bwd[None],
        saved_pre[0, 0], w_up[0], w_down[0], basis_q.T,
    )
    return (expert_out, grad_in, left.T[None], right.T[None, None])


def solution(mesh):
    def choose(*arguments):
        n = lax.axis_size("expert")
        capacity = arguments[0].shape[0] // (n // 2)
        rank = arguments[9].shape[1]
        whole_tiles = capacity % 16 == 0 and rank % 32 == 0
        pairs = lax.axis_size("dp") == 2 and lax.axis_size("section") % 2 == 0
        return (fused_body if whole_tiles and pairs else body)(*arguments)

    return jax.shard_map(
        choose,
        mesh=mesh,
        in_specs=(
            P(("section", "expert", "dp"), None),
            P(("section", "expert", "dp")),
            P(("section", "expert", "dp")),
            P(("section", "expert", "dp"), None),
            P(("section", "expert", "dp")),
            P(("section", "expert", "dp")),
            P("section", "dp", None, "expert"),
            P("section", None, "expert"),
            P("section", "expert", None),
            P(),
        ),
        out_specs=(
            P(("section", "expert", "dp"), None),
            P(("section", "expert", "dp"), None),
            P("section", "expert", None),
            P("section", "expert", None, None),
        ),
        check_vma=False,
    )
```

```python
import functools

import jax
import jax.numpy as jnp
from jax import lax
from jax.experimental import pallas as pl
from jax.experimental.pallas import tpu as pltpu
from jax.sharding import PartitionSpec as P

highest = lax.Precision.HIGHEST
MESH = pl.DeviceIdType.MESH
BLOCK = 16
VMEM_LIMIT = 63 * 2**20


def from_partner(value, axis, apart):
    mask = 2**apart
    pairs = [(source, source ^ mask) for source in range(lax.axis_size(axis))]
    return lax.ppermute(value, axis, pairs)


def orthonormal(matrix):
    column_count = matrix.shape[1]

    def place_column(position, result):
        column = lax.dynamic_slice_in_dim(matrix, position, 1, 1)
        earlier = (jnp.arange(column_count, dtype=jnp.int32) < position).astype(matrix.dtype)[
            :, None
        ]
        for repeat in range(2):
            project = jnp.dot(result.T, column, precision=highest) * earlier
            column = column - jnp.dot(result, project, precision=highest)
        column = column * lax.rsqrt(jnp.sum(column * column) + 1e-06)
        return lax.dynamic_update_slice_in_dim(result, column, position, 1)

    return lax.fori_loop(0, column_count, place_column, jnp.zeros_like(matrix))


def contract_last(left, right):
    return lax.dot_general(
        left, right, (((1,), (1,)), ((), ())), preferred_element_type=jnp.float32
    )


def spread_rows(picked):
    device_count = lax.axis_size("expert")
    experts_live = picked.shape[0]
    capacity = picked.shape[1]
    features = picked.shape[2]
    return jnp.broadcast_to(picked[:, None], (experts_live, 2, capacity, features)).reshape(
        device_count, capacity, features
    )


def send_rows(first_picked, second_picked):
    first_out = spread_rows(first_picked)
    second_out = spread_rows(second_picked)
    first_arrived, second_arrived = [
        lax.all_to_all(element, "expert", split_axis=0, concat_axis=0, tiled=True)
        for element in (first_out, second_out)
    ]
    features = first_arrived.shape[2]
    return (first_arrived.reshape(-1, features), second_arrived.reshape(-1, features))


def collect_rows(returned, experts_live):
    features = returned.shape[2]
    capacity = returned.shape[1]
    summed = returned.reshape(experts_live, 2, capacity, features).astype(jnp.float32)
    return (summed[:, 0] + summed[:, 1]).astype(jnp.bfloat16).reshape(-1, features)


def send_back(first_partial, second_partial, experts_live):
    device_count = lax.axis_size("expert")
    features = first_partial.shape[1]
    capacity = first_partial.shape[0] // device_count
    first_out = first_partial.reshape(device_count, capacity, features).astype(jnp.bfloat16)
    second_out = second_partial.reshape(device_count, capacity, features).astype(jnp.bfloat16)
    first_returned, second_returned = [
        lax.all_to_all(element, "expert", split_axis=0, concat_axis=0, tiled=True)
        for element in (first_out, second_out)
    ]
    return (collect_rows(first_returned, experts_live), collect_rows(second_returned, experts_live))


def pair_total(local_term):
    mirrored = local_term
    for bit_level in range(lax.axis_size("section").bit_length() - 1):
        mirrored = from_partner(mirrored, "section", bit_level)
    return lax.psum(local_term + mirrored, "dp")


def body(
    tokens_fwd, route_fwd, gate_fwd, grad_out, route_bwd, gate_bwd, saved_pre, w_up, w_down, basis_q
):
    device_count = lax.axis_size("expert")
    experts_live = device_count // 2
    token_count = tokens_fwd.shape[0]
    features = tokens_fwd.shape[1]
    capacity = token_count // experts_live
    up_cols = w_up[0]
    down_rows = w_down[0]
    order_fwd = jnp.argsort(route_fwd, stable=True)
    inverse_fwd = jnp.argsort(order_fwd)
    scaled = (gate_bwd[:, None] * grad_out.astype(jnp.float32)).astype(jnp.bfloat16)
    order_bwd = jnp.argsort(route_bwd, stable=True)
    inverse_bwd = jnp.argsort(order_bwd)
    inputs, grad_rows = send_rows(
        tokens_fwd[order_fwd].reshape(experts_live, capacity, features),
        scaled[order_bwd].reshape(experts_live, capacity, features),
    )
    hidden = jax.nn.silu(jnp.dot(inputs, up_cols, preferred_element_type=jnp.float32)).astype(
        jnp.bfloat16
    )
    partial_value = jnp.dot(hidden, down_rows, preferred_element_type=jnp.float32)
    preact = saved_pre[0, 0].astype(jnp.float32)
    sigmoid_pre = jax.nn.sigmoid(preact)
    hidden_bwd = (preact * sigmoid_pre).astype(jnp.bfloat16)
    slope_term = sigmoid_pre * (1.0 + preact * (1.0 - sigmoid_pre))
    pre_grad = (contract_last(grad_rows, down_rows) * slope_term).astype(jnp.bfloat16)
    input_part = contract_last(pre_grad, up_cols)
    mixed_sorted, grad_sorted = send_back(partial_value, input_part, experts_live)
    expert_out = (gate_fwd[:, None] * mixed_sorted[inverse_fwd].astype(jnp.float32)).astype(
        jnp.bfloat16
    )
    grad_in = grad_sorted[inverse_bwd]
    weight_grad = lax.dot_general(
        hidden_bwd, grad_rows, (((0,), (0,)), ((), ())), preferred_element_type=jnp.float32
    )
    left_term = jnp.dot(weight_grad, basis_q, precision=highest)
    left_factor = orthonormal(pair_total(left_term))
    right_term = lax.dot_general(
        weight_grad,
        left_factor,
        (((0,), (0,)), ((), ())),
        precision=highest,
        preferred_element_type=jnp.float32,
    )
    right_factor = pair_total(right_term).astype(jnp.bfloat16)
    return (expert_out, grad_in, left_factor[None], right_factor[None, None])


def slot_matrix(route_row, capacity):
    count = route_row.shape[1]
    first = lax.broadcasted_iota(jnp.int32, (count, count), 0)
    second = lax.broadcasted_iota(jnp.int32, (count, count), 1)
    across = jnp.broadcast_to(route_row.astype(jnp.float32), (count, count))
    down = jnp.sum(jnp.where(first == second, across, 0.0), axis=1, keepdims=True)
    ahead = jnp.where((down == across) & (first < second), 1.0, 0.0)
    slot = across * capacity + jnp.sum(ahead, axis=0, keepdims=True)
    return jnp.where(slot == first.astype(jnp.float32), 1.0, 0.0).astype(jnp.bfloat16)


def as_column(row):
    count = row.shape[1]
    first = lax.broadcasted_iota(jnp.int32, (count, count), 0)
    second = lax.broadcasted_iota(jnp.int32, (count, count), 1)
    return jnp.sum(jnp.where(first == second, row, 0.0), axis=1, keepdims=True)


def halves(value):
    high = value.astype(jnp.bfloat16)
    return high, (value - high.astype(jnp.float32)).astype(jnp.bfloat16)


def dot32(left, right, dims=((1,), (0,))):
    return lax.dot_general(left, right, (dims, ((), ())), preferred_element_type=jnp.float32)


def fused_kernel(
    sizes,
    tok_hbm, rf_ref, gf_ref, go_hbm, rb_ref, gb_ref, pre_hbm, up_hbm, down_hbm, basis_hbm,
    out_ref, gin_ref, p_ref, q_ref,
    tok_ref, go_ref, pre_ref, up, down, basis, sendz, sendx, zbuf, xbuf, partb, partf, retb, retf,
    lown, lpeer, lsum, lpart, amat, umat, rown, rpeer, rsum, zout, zin, qbuf,
    hb_ref, slope_ref, terms, terms_in,
    local_sem, zs, zr, xs, xr, bs, br, fs, fr, ts, tr, ps, pr,
):
    n, n_sec, cap = sizes
    live = n // 2
    me = lax.axis_index("expert")
    core = lax.axis_index("dp")
    sibling = {"dp": 1 - core}
    mirror = {"section": n_sec - 1 - lax.axis_index("section")}

    loads = [
        pltpu.make_async_copy(source, target, local_sem.at[i])
        for i, (source, target) in enumerate(
            (
                (go_hbm, go_ref), (basis_hbm, basis), (tok_hbm, tok_ref),
                (pre_hbm, pre_ref), (down_hbm, down), (up_hbm, up),
            )
        )
    ]
    for load in loads:
        load.start()

    barrier = pltpu.get_barrier_semaphore()
    for shift in range(1, n):
        pl.semaphore_signal(
            barrier, inc=1, device_id={"expert": lax.rem(me + shift, n)}, device_id_type=MESH
        )
    pl.semaphore_signal(barrier, inc=1, device_id=sibling, device_id_type=MESH)
    pl.semaphore_signal(barrier, inc=1, device_id=mirror, device_id_type=MESH)

    def rows_of(index):
        return pl.ds(pl.multiple_of(index * cap, cap), cap)

    def remote(source, target, send, recv, device):
        return pltpu.make_async_remote_copy(
            src_ref=source, dst_ref=target, send_sem=send, recv_sem=recv,
            device_id=device, device_id_type=MESH,
        )

    def dispatch(source, target, send, recv):
        copies = []
        for shift in range(1, n):
            to = lax.rem(me + shift, n)
            copies.append(
                remote(source.at[rows_of(to // 2)], target.at[rows_of(me)],
                       send.at[shift], recv.at[shift], {"expert": to})
            )
        for copy in copies:
            copy.start()
        target[rows_of(me)] = source[rows_of(me // 2)]
        return copies

    def send_back(source, target, send, recv):
        copies = []
        for shift in range(1, n):
            to = lax.rem(me + shift, n)
            copies.append(
                remote(source.at[rows_of(to)], target.at[rows_of(me)],
                       send.at[shift], recv.at[shift], {"expert": to})
            )
        for copy in copies:
            copy.start()
        target[rows_of(me)] = source[rows_of(me)]
        return copies

    def combine(returned):
        sums = [
            (
                returned[2 * e * cap : (2 * e + 1) * cap].astype(jnp.float32)
                + returned[(2 * e + 1) * cap : (2 * e + 2) * cap].astype(jnp.float32)
            ).astype(jnp.bfloat16)
            for e in range(live)
        ]
        return jnp.concatenate(sums, axis=0)

    place_bwd = slot_matrix(rb_ref[...], cap)
    loads[0].wait()
    scaled = (as_column(gb_ref[...]) * go_ref[...].astype(jnp.float32)).astype(jnp.bfloat16)
    sendz[...] = dot32(place_bwd, scaled).astype(jnp.bfloat16)
    loads[1].wait()
    basis_high, basis_low = halves(basis[...])
    nt = ((1,), (1,))
    terms[...] = dot32(sendz[...], basis_high, nt) + dot32(sendz[...], basis_low, nt)
    pl.semaphore_wait(barrier, n + 1)
    t_copies = dispatch(terms, terms_in, ts, tr)
    z_copies = dispatch(sendz, zbuf, zs, zr)
    place_fwd = slot_matrix(rf_ref[...], cap)
    loads[2].wait()
    sendx[...] = dot32(place_fwd, tok_ref[...]).astype(jnp.bfloat16)
    x_copies = dispatch(sendx, xbuf, xs, xr)

    loads[3].wait()
    preact = pre_ref[...].astype(jnp.float32)
    sigmoid = jax.nn.sigmoid(preact)
    hb_ref[...] = (preact * sigmoid).astype(jnp.bfloat16)

    for copy in t_copies:
        copy.wait()
    zb_high, zb_low = halves(terms_in[...].T)
    lown[...] = dot32(zb_high, hb_ref[...]) + dot32(zb_low, hb_ref[...])
    left_dp = remote(lown, lpeer, ps.at[0], pr.at[0], sibling)
    left_dp.start()
    slope_ref[...] = sigmoid * (1.0 + preact * (1.0 - sigmoid))
    umat[...] = jnp.zeros_like(umat)
    left_dp.wait()
    lsum[...] = lown[...] + lpeer[...]
    left_z = remote(lsum, lpart, ps.at[1], pr.at[1], mirror)
    left_z.start()
    left_z.wait()
    amat[...] = lsum[...] + lpart[...]
    rank = amat.shape[0]
    features = rown.shape[1]
    span = features // 2
    mine = pl.ds(pl.multiple_of(core * span, 128), span)
    other = pl.ds(pl.multiple_of((1 - core) * span, 128), span)

    def place(reach, k, v):
        earlier = umat[0:reach]
        follow = amat[pl.ds(lax.rem(k + 1, rank), 1), :]
        again = jnp.sum(earlier * v, axis=1, keepdims=True)
        ahead = jnp.sum(earlier * follow, axis=1, keepdims=True)
        v = v - jnp.sum(earlier * again, axis=0, keepdims=True)
        follow_left = follow - jnp.sum(earlier * ahead, axis=0, keepdims=True)
        square = jnp.sum(v * v, axis=1, keepdims=True)
        share = jnp.sum(v * follow, axis=1, keepdims=True)
        inverse = lax.rsqrt(square + 1e-06)
        unit = v * inverse
        umat[pl.ds(k, 1), :] = unit
        return follow_left - unit * (share * inverse)

    def columns(block):
        return slice(block * BLOCK, (block + 1) * BLOCK)

    def both(high, low):
        return jnp.concatenate([high, low], axis=0)

    def right_copies(block):
        rows, first = pl.ds(block * BLOCK, BLOCK), 2 + 3 * block
        return (
            remote(rown.at[rows, other], rpeer.at[rows], ps.at[first], pr.at[first], sibling),
            remote(zout.at[rows], zin.at[rows], ps.at[first + 1], pr.at[first + 1], mirror),
            remote(qbuf.at[rows, mine], qbuf.at[rows, mine],
                   ps.at[first + 2], pr.at[first + 2], sibling),
        )

    def right_begin(block):
        hp = dot32(both(*halves(umat[columns(block)])), hb_ref[...], nt)
        right = dot32(both(*halves(hp[:BLOCK] + hp[BLOCK:])), zbuf[...])
        rown[columns(block)] = right[:BLOCK] + right[BLOCK:]
        rights[block][0].start()

    def right_mirror(block):
        rights[block][0].wait()
        rsum[columns(block)] = rown[columns(block), mine] + rpeer[columns(block)]
        zout[columns(block)] = rsum[columns(block)].astype(jnp.bfloat16)
        rights[block][1].start()

    def right_share(block):
        rights[block][1].wait()
        total = rsum[columns(block)] + zin[columns(block)].astype(jnp.float32)
        qbuf[columns(block), mine] = total.astype(jnp.bfloat16)
        rights[block][2].start()

    blocks = rank // BLOCK
    rights = [right_copies(block) for block in range(blocks)]
    v = amat[pl.ds(0, 1), :]
    for block in range(blocks):
        middle, top = block * BLOCK + BLOCK // 2, (block + 1) * BLOCK
        v = lax.fori_loop(block * BLOCK, middle, functools.partial(place, middle), v)
        if block >= 1:
            right_mirror(block - 1)
        v = lax.fori_loop(middle, top, functools.partial(place, top), v)
        if block == 0:
            for copy in z_copies:
                copy.wait()
        right_begin(block)
        if block >= 1:
            right_share(block - 1)
        if block == 0:
            loads[4].wait()
            pre_grad = dot32(zbuf[...], down[...], nt) * slope_ref[...]
            loads[5].wait()
            partb[...] = dot32(pre_grad.astype(jnp.bfloat16), up[...], nt).astype(jnp.bfloat16)
            b_copies = send_back(partb, retb, bs, br)
        if block == min(1, blocks - 1):
            for copy in x_copies:
                copy.wait()
            value = dot32(xbuf[...], up[...])
            hidden = (value * jax.nn.sigmoid(value)).astype(jnp.bfloat16)
            partf[...] = dot32(hidden, down[...]).astype(jnp.bfloat16)
            f_copies = send_back(partf, retf, fs, fr)
    for copy in b_copies:
        copy.wait()
    gin_ref[...] = dot32(place_bwd, combine(retb), ((0,), (0,))).astype(jnp.bfloat16)
    right_mirror(blocks - 1)
    p_ref[...] = umat[...]
    for copy in f_copies:
        copy.wait()
    mixed = dot32(place_fwd, combine(retf), ((0,), (0,)))
    out_ref[...] = (as_column(gf_ref[...]) * mixed).astype(jnp.bfloat16)
    right_share(blocks - 1)
    for copies in rights:
        copies[2].wait()
    q_ref[...] = qbuf[...]


def finish_kernel(*refs):
    count = len(refs) // 2
    copies = [
        pltpu.make_async_copy(refs[i], refs[count + i], refs[-1].at[i]) for i in range(count)
    ]
    for copy in copies:
        copy.start()
    for copy in copies:
        copy.wait()


def finish(arrays):
    return pl.pallas_call(
        finish_kernel,
        out_shape=tuple(jax.ShapeDtypeStruct(a.shape, a.dtype) for a in arrays),
        in_specs=[pl.BlockSpec(memory_space=pl.ANY)] * len(arrays),
        out_specs=(pl.BlockSpec(memory_space=pltpu.VMEM),) * len(arrays),
        scratch_shapes=[pltpu.SemaphoreType.DMA((len(arrays),))],
        compiler_params=pltpu.CompilerParams(vmem_limit_bytes=VMEM_LIMIT),
    )(*arrays)


def fused_body(
    tokens_fwd, route_fwd, gate_fwd, grad_out, route_bwd, gate_bwd, saved_pre, w_up, w_down, basis_q
):
    n, n_sec = lax.axis_size("expert"), lax.axis_size("section")
    count, features = tokens_fwd.shape
    cap = count // (n // 2)
    slots, units = saved_pre.shape[2:]
    rank = basis_q.shape[1]
    bf, f32 = jnp.bfloat16, jnp.float32
    vmem = pl.BlockSpec(memory_space=pltpu.VMEM)
    hbm = pl.BlockSpec(memory_space=pltpu.HBM)
    wide = [pltpu.VMEM((slots, features), bf)]
    square = [pltpu.VMEM((rank, units), f32)]
    half = (rank, features // 2)
    results = pl.pallas_call(
        functools.partial(fused_kernel, (n, n_sec, cap)),
        out_shape=(
            jax.ShapeDtypeStruct((count, features), bf),
            jax.ShapeDtypeStruct((count, features), bf),
            jax.ShapeDtypeStruct((rank, units), f32),
            jax.ShapeDtypeStruct((rank, features), bf),
        ),
        in_specs=[hbm, vmem, vmem, hbm, vmem, vmem, hbm, hbm, hbm, hbm],
        out_specs=(vmem,) * 4,
        scratch_shapes=[
            pltpu.VMEM((count, features), bf),
            pltpu.VMEM((count, features), bf),
            pltpu.VMEM((slots, units), bf),
            pltpu.VMEM((features, units), bf),
            pltpu.VMEM((units, features), bf),
            pltpu.VMEM((rank, features), f32),
            pltpu.VMEM((count, features), bf),
            pltpu.VMEM((count, features), bf),
        ]
        + wide * 4
        + [pltpu.VMEM((n * cap, features), bf)] * 2
        + square * 6
        + [
            pltpu.VMEM((rank, features), f32),
            pltpu.VMEM(half, f32),
            pltpu.VMEM(half, f32),
            pltpu.VMEM(half, bf),
            pltpu.VMEM(half, bf),
            pltpu.VMEM((rank, features), bf),
            pltpu.VMEM((slots, units), bf),
            pltpu.VMEM((slots, units), f32),
            pltpu.VMEM((count, rank), f32),
            pltpu.VMEM((slots, rank), f32),
            pltpu.SemaphoreType.DMA((6,)),
        ]
        + [pltpu.SemaphoreType.DMA((n,))] * 10
        + [pltpu.SemaphoreType.DMA((2 + 3 * (rank // BLOCK),))] * 2,
        compiler_params=pltpu.CompilerParams(
            collective_id=0, has_side_effects=True, vmem_limit_bytes=VMEM_LIMIT
        ),
    )(
        tokens_fwd, route_fwd[None], gate_fwd[None], grad_out, route_bwd[None], gate_bwd[None],
        saved_pre[0, 0], w_up[0], w_down[0], basis_q.T,
    )
    expert_out, grad_in, left, right = finish(results)
    return (expert_out, grad_in, left.T[None], right.T[None, None])


def solution(mesh):
    def choose(*arguments):
        n = lax.axis_size("expert")
        capacity = arguments[0].shape[0] // (n // 2)
        rank = arguments[9].shape[1]
        whole_tiles = capacity % 16 == 0 and rank % BLOCK == 0
        whole_tiles = whole_tiles and arguments[0].shape[1] % 256 == 0
        pairs = lax.axis_size("dp") == 2 and lax.axis_size("section") % 2 == 0
        return (fused_body if whole_tiles and pairs else body)(*arguments)

    return jax.shard_map(
        choose,
        mesh=mesh,
        in_specs=(
            P(("section", "expert", "dp"), None),
            P(("section", "expert", "dp")),
            P(("section", "expert", "dp")),
            P(("section", "expert", "dp"), None),
            P(("section", "expert", "dp")),
            P(("section", "expert", "dp")),
            P("section", "dp", None, "expert"),
            P("section", None, "expert"),
            P("section", "expert", None),
            P(),
        ),
        out_specs=(
            P(("section", "expert", "dp"), None),
            P(("section", "expert", "dp"), None),
            P("section", "expert", None),
            P("section", "expert", None, None),
        ),
        check_vma=False,
    )
```

```python
import functools

import jax
import jax.numpy as jnp
from jax import lax
from jax.experimental import pallas as pl
from jax.experimental.pallas import tpu as pltpu
from jax.sharding import PartitionSpec as P

highest = lax.Precision.HIGHEST
MESH = pl.DeviceIdType.MESH
BLOCK = 16
VMEM_LIMIT = 63 * 2**20


def from_partner(value, axis, apart):
    mask = 2**apart
    pairs = [(source, source ^ mask) for source in range(lax.axis_size(axis))]
    return lax.ppermute(value, axis, pairs)


def orthonormal(matrix):
    column_count = matrix.shape[1]

    def place_column(position, result):
        column = lax.dynamic_slice_in_dim(matrix, position, 1, 1)
        earlier = (jnp.arange(column_count, dtype=jnp.int32) < position).astype(matrix.dtype)[
            :, None
        ]
        for repeat in range(2):
            project = jnp.dot(result.T, column, precision=highest) * earlier
            column = column - jnp.dot(result, project, precision=highest)
        column = column * lax.rsqrt(jnp.sum(column * column) + 1e-06)
        return lax.dynamic_update_slice_in_dim(result, column, position, 1)

    return lax.fori_loop(0, column_count, place_column, jnp.zeros_like(matrix))


def contract_last(left, right):
    return lax.dot_general(
        left, right, (((1,), (1,)), ((), ())), preferred_element_type=jnp.float32
    )


def spread_rows(picked):
    device_count = lax.axis_size("expert")
    experts_live = picked.shape[0]
    capacity = picked.shape[1]
    features = picked.shape[2]
    return jnp.broadcast_to(picked[:, None], (experts_live, 2, capacity, features)).reshape(
        device_count, capacity, features
    )


def send_rows(first_picked, second_picked):
    first_out = spread_rows(first_picked)
    second_out = spread_rows(second_picked)
    first_arrived, second_arrived = [
        lax.all_to_all(element, "expert", split_axis=0, concat_axis=0, tiled=True)
        for element in (first_out, second_out)
    ]
    features = first_arrived.shape[2]
    return (first_arrived.reshape(-1, features), second_arrived.reshape(-1, features))


def collect_rows(returned, experts_live):
    features = returned.shape[2]
    capacity = returned.shape[1]
    summed = returned.reshape(experts_live, 2, capacity, features).astype(jnp.float32)
    return (summed[:, 0] + summed[:, 1]).astype(jnp.bfloat16).reshape(-1, features)


def send_back(first_partial, second_partial, experts_live):
    device_count = lax.axis_size("expert")
    features = first_partial.shape[1]
    capacity = first_partial.shape[0] // device_count
    first_out = first_partial.reshape(device_count, capacity, features).astype(jnp.bfloat16)
    second_out = second_partial.reshape(device_count, capacity, features).astype(jnp.bfloat16)
    first_returned, second_returned = [
        lax.all_to_all(element, "expert", split_axis=0, concat_axis=0, tiled=True)
        for element in (first_out, second_out)
    ]
    return (collect_rows(first_returned, experts_live), collect_rows(second_returned, experts_live))


def pair_total(local_term):
    mirrored = local_term
    for bit_level in range(lax.axis_size("section").bit_length() - 1):
        mirrored = from_partner(mirrored, "section", bit_level)
    return lax.psum(local_term + mirrored, "dp")


def body(
    tokens_fwd, route_fwd, gate_fwd, grad_out, route_bwd, gate_bwd, saved_pre, w_up, w_down, basis_q
):
    device_count = lax.axis_size("expert")
    experts_live = device_count // 2
    token_count = tokens_fwd.shape[0]
    features = tokens_fwd.shape[1]
    capacity = token_count // experts_live
    up_cols = w_up[0]
    down_rows = w_down[0]
    order_fwd = jnp.argsort(route_fwd, stable=True)
    inverse_fwd = jnp.argsort(order_fwd)
    scaled = (gate_bwd[:, None] * grad_out.astype(jnp.float32)).astype(jnp.bfloat16)
    order_bwd = jnp.argsort(route_bwd, stable=True)
    inverse_bwd = jnp.argsort(order_bwd)
    inputs, grad_rows = send_rows(
        tokens_fwd[order_fwd].reshape(experts_live, capacity, features),
        scaled[order_bwd].reshape(experts_live, capacity, features),
    )
    hidden = jax.nn.silu(jnp.dot(inputs, up_cols, preferred_element_type=jnp.float32)).astype(
        jnp.bfloat16
    )
    partial_value = jnp.dot(hidden, down_rows, preferred_element_type=jnp.float32)
    preact = saved_pre[0, 0].astype(jnp.float32)
    sigmoid_pre = jax.nn.sigmoid(preact)
    hidden_bwd = (preact * sigmoid_pre).astype(jnp.bfloat16)
    slope_term = sigmoid_pre * (1.0 + preact * (1.0 - sigmoid_pre))
    pre_grad = (contract_last(grad_rows, down_rows) * slope_term).astype(jnp.bfloat16)
    input_part = contract_last(pre_grad, up_cols)
    mixed_sorted, grad_sorted = send_back(partial_value, input_part, experts_live)
    expert_out = (gate_fwd[:, None] * mixed_sorted[inverse_fwd].astype(jnp.float32)).astype(
        jnp.bfloat16
    )
    grad_in = grad_sorted[inverse_bwd]
    weight_grad = lax.dot_general(
        hidden_bwd, grad_rows, (((0,), (0,)), ((), ())), preferred_element_type=jnp.float32
    )
    left_term = jnp.dot(weight_grad, basis_q, precision=highest)
    left_factor = orthonormal(pair_total(left_term))
    right_term = lax.dot_general(
        weight_grad,
        left_factor,
        (((0,), (0,)), ((), ())),
        precision=highest,
        preferred_element_type=jnp.float32,
    )
    right_factor = pair_total(right_term).astype(jnp.bfloat16)
    return (expert_out, grad_in, left_factor[None], right_factor[None, None])


def slot_matrix(route_row, capacity):
    count = route_row.shape[1]
    first = lax.broadcasted_iota(jnp.int32, (count, count), 0)
    second = lax.broadcasted_iota(jnp.int32, (count, count), 1)
    across = jnp.broadcast_to(route_row.astype(jnp.float32), (count, count))
    down = jnp.sum(jnp.where(first == second, across, 0.0), axis=1, keepdims=True)
    ahead = jnp.where((down == across) & (first < second), 1.0, 0.0)
    slot = across * capacity + jnp.sum(ahead, axis=0, keepdims=True)
    return jnp.where(slot == first.astype(jnp.float32), 1.0, 0.0).astype(jnp.bfloat16)


def as_column(row):
    count = row.shape[1]
    first = lax.broadcasted_iota(jnp.int32, (count, count), 0)
    second = lax.broadcasted_iota(jnp.int32, (count, count), 1)
    return jnp.sum(jnp.where(first == second, row, 0.0), axis=1, keepdims=True)


def halves(value):
    high = value.astype(jnp.bfloat16)
    return high, (value - high.astype(jnp.float32)).astype(jnp.bfloat16)


def dot32(left, right, dims=((1,), (0,))):
    return lax.dot_general(left, right, (dims, ((), ())), preferred_element_type=jnp.float32)


def fused_kernel(
    sizes,
    tok_hbm, rf_ref, gf_ref, go_hbm, rb_ref, gb_ref, pre_hbm, up_hbm, down_hbm, basis_hbm,
    out_ref, gin_ref, p_ref, q_ref,
    tok_ref, go_ref, pre_ref, up, down, basis, sendz, sendx, zbuf, xbuf, partb, partf, retb, retf,
    lown, lpeer, lsum, lpart, amat, umat, rown, rpeer, rsum, zout, zin, qbuf,
    hb_ref, slope_ref, terms, terms_in,
    local_sem, zs, zr, xs, xr, bs, br, fs, fr, ts, tr, ps, pr,
):
    n, n_sec, cap = sizes
    live = n // 2
    me = lax.axis_index("expert")
    core = lax.axis_index("dp")
    sibling = {"dp": 1 - core}
    mirror = {"section": n_sec - 1 - lax.axis_index("section")}

    loads = [
        pltpu.make_async_copy(source, target, local_sem.at[i])
        for i, (source, target) in enumerate(
            (
                (go_hbm, go_ref), (basis_hbm, basis), (tok_hbm, tok_ref),
                (pre_hbm, pre_ref), (down_hbm, down), (up_hbm, up),
            )
        )
    ]
    for load in loads:
        load.start()

    barrier = pltpu.get_barrier_semaphore()
    for shift in range(1, n):
        pl.semaphore_signal(
            barrier, inc=1, device_id={"expert": lax.rem(me + shift, n)}, device_id_type=MESH
        )
    pl.semaphore_signal(barrier, inc=1, device_id=sibling, device_id_type=MESH)
    pl.semaphore_signal(barrier, inc=1, device_id=mirror, device_id_type=MESH)

    def rows_of(index):
        return pl.ds(pl.multiple_of(index * cap, cap), cap)

    def remote(source, target, send, recv, device):
        return pltpu.make_async_remote_copy(
            src_ref=source, dst_ref=target, send_sem=send, recv_sem=recv,
            device_id=device, device_id_type=MESH,
        )

    def dispatch(source, target, send, recv):
        copies = []
        for shift in range(1, n):
            to = lax.rem(me + shift, n)
            copies.append(
                remote(source.at[rows_of(to // 2)], target.at[rows_of(me)],
                       send.at[shift], recv.at[shift], {"expert": to})
            )
        for copy in copies:
            copy.start()
        target[rows_of(me)] = source[rows_of(me // 2)]
        return copies

    def send_back(source, target, send, recv):
        copies = []
        for shift in range(1, n):
            to = lax.rem(me + shift, n)
            copies.append(
                remote(source.at[rows_of(to)], target.at[rows_of(me)],
                       send.at[shift], recv.at[shift], {"expert": to})
            )
        for copy in copies:
            copy.start()
        target[rows_of(me)] = source[rows_of(me)]
        return copies

    def combine(returned):
        sums = [
            (
                returned[2 * e * cap : (2 * e + 1) * cap].astype(jnp.float32)
                + returned[(2 * e + 1) * cap : (2 * e + 2) * cap].astype(jnp.float32)
            ).astype(jnp.bfloat16)
            for e in range(live)
        ]
        return jnp.concatenate(sums, axis=0)

    place_bwd = slot_matrix(rb_ref[...], cap)
    loads[0].wait()
    scaled = (as_column(gb_ref[...]) * go_ref[...].astype(jnp.float32)).astype(jnp.bfloat16)
    sendz[...] = dot32(place_bwd, scaled).astype(jnp.bfloat16)
    loads[1].wait()
    basis_high, basis_low = halves(basis[...])
    nt = ((1,), (1,))
    terms[...] = dot32(sendz[...], basis_high, nt) + dot32(sendz[...], basis_low, nt)
    pl.semaphore_wait(barrier, n + 1)
    t_copies = dispatch(terms, terms_in, ts, tr)
    z_copies = dispatch(sendz, zbuf, zs, zr)
    place_fwd = slot_matrix(rf_ref[...], cap)
    loads[2].wait()
    sendx[...] = dot32(place_fwd, tok_ref[...]).astype(jnp.bfloat16)
    x_copies = dispatch(sendx, xbuf, xs, xr)

    loads[3].wait()
    preact = pre_ref[...].astype(jnp.float32)
    sigmoid = jax.nn.sigmoid(preact)
    hb_ref[...] = (preact * sigmoid).astype(jnp.bfloat16)

    for copy in t_copies:
        copy.wait()
    zb_high, zb_low = halves(terms_in[...].T)
    lown[...] = dot32(zb_high, hb_ref[...]) + dot32(zb_low, hb_ref[...])
    left_dp = remote(lown, lpeer, ps.at[0], pr.at[0], sibling)
    left_dp.start()
    slope_ref[...] = sigmoid * (1.0 + preact * (1.0 - sigmoid))
    umat[...] = jnp.zeros_like(umat)
    left_dp.wait()
    lsum[...] = lown[...] + lpeer[...]
    rank = amat.shape[0]
    blocks = rank // BLOCK
    lefts = [
        remote(lsum.at[pl.ds(block * BLOCK, BLOCK)], lpart.at[pl.ds(block * BLOCK, BLOCK)],
               ps.at[1 + block], pr.at[1 + block], mirror)
        for block in range(blocks)
    ]
    for copy in lefts:
        copy.start()

    def left_arrives(block):
        lefts[block].wait()
        rows = slice(block * BLOCK, (block + 1) * BLOCK)
        amat[rows] = lsum[rows] + lpart[rows]

    features = rown.shape[1]
    span = features // 2
    mine = pl.ds(pl.multiple_of(core * span, 128), span)
    other = pl.ds(pl.multiple_of((1 - core) * span, 128), span)

    def place(reach, k, v):
        earlier = umat[0:reach]
        follow = amat[pl.ds(lax.rem(k + 1, rank), 1), :]
        again = jnp.sum(earlier * v, axis=1, keepdims=True)
        ahead = jnp.sum(earlier * follow, axis=1, keepdims=True)
        v = v - jnp.sum(earlier * again, axis=0, keepdims=True)
        follow_left = follow - jnp.sum(earlier * ahead, axis=0, keepdims=True)
        square = jnp.sum(v * v, axis=1, keepdims=True)
        share = jnp.sum(v * follow, axis=1, keepdims=True)
        inverse = lax.rsqrt(square + 1e-06)
        unit = v * inverse
        umat[pl.ds(k, 1), :] = unit
        return follow_left - unit * (share * inverse)

    def columns(block):
        return slice(block * BLOCK, (block + 1) * BLOCK)

    def both(high, low):
        return jnp.concatenate([high, low], axis=0)

    def right_copies(block):
        rows, first = pl.ds(block * BLOCK, BLOCK), 1 + blocks + 3 * block
        return (
            remote(rown.at[rows, other], rpeer.at[rows], ps.at[first], pr.at[first], sibling),
            remote(zout.at[rows], zin.at[rows], ps.at[first + 1], pr.at[first + 1], mirror),
            remote(qbuf.at[rows, mine], qbuf.at[rows, mine],
                   ps.at[first + 2], pr.at[first + 2], sibling),
        )

    def right_begin(block):
        hp = dot32(both(*halves(umat[columns(block)])), hb_ref[...], nt)
        right = dot32(both(*halves(hp[:BLOCK] + hp[BLOCK:])), zbuf[...])
        rown[columns(block)] = right[:BLOCK] + right[BLOCK:]
        rights[block][0].start()

    def right_mirror(block):
        rights[block][0].wait()
        rsum[columns(block)] = rown[columns(block), mine] + rpeer[columns(block)]
        zout[columns(block)] = rsum[columns(block)].astype(jnp.bfloat16)
        rights[block][1].start()

    def right_share(block):
        rights[block][1].wait()
        total = rsum[columns(block)] + zin[columns(block)].astype(jnp.float32)
        qbuf[columns(block), mine] = total.astype(jnp.bfloat16)
        rights[block][2].start()

    rights = [right_copies(block) for block in range(blocks)]
    left_arrives(0)
    v = amat[pl.ds(0, 1), :]
    for block in range(blocks):
        middle, top = block * BLOCK + BLOCK // 2, (block + 1) * BLOCK
        v = lax.fori_loop(block * BLOCK, middle, functools.partial(place, middle), v)
        if block >= 1:
            right_mirror(block - 1)
        if block >= 2:
            right_share(block - 2)
        if block + 1 < blocks:
            left_arrives(block + 1)
        v = lax.fori_loop(middle, top, functools.partial(place, top), v)
        if block == 0:
            for copy in z_copies:
                copy.wait()
        right_begin(block)
        if block == 0:
            loads[4].wait()
            pre_grad = dot32(zbuf[...], down[...], nt) * slope_ref[...]
            loads[5].wait()
            partb[...] = dot32(pre_grad.astype(jnp.bfloat16), up[...], nt).astype(jnp.bfloat16)
            b_copies = send_back(partb, retb, bs, br)
        if block == min(1, blocks - 1):
            for copy in x_copies:
                copy.wait()
            value = dot32(xbuf[...], up[...])
            hidden = (value * jax.nn.sigmoid(value)).astype(jnp.bfloat16)
            partf[...] = dot32(hidden, down[...]).astype(jnp.bfloat16)
            f_copies = send_back(partf, retf, fs, fr)
    for copy in b_copies:
        copy.wait()
    gin_ref[...] = dot32(place_bwd, combine(retb), ((0,), (0,))).astype(jnp.bfloat16)
    right_mirror(blocks - 1)
    p_ref[...] = umat[...]
    for copy in f_copies:
        copy.wait()
    mixed = dot32(place_fwd, combine(retf), ((0,), (0,)))
    out_ref[...] = (as_column(gf_ref[...]) * mixed).astype(jnp.bfloat16)
    if blocks >= 2:
        right_share(blocks - 2)
    right_share(blocks - 1)
    for copies in rights:
        copies[2].wait()
    q_ref[...] = qbuf[...]


def finish_kernel(*refs):
    count = len(refs) // 2
    copies = [
        pltpu.make_async_copy(refs[i], refs[count + i], refs[-1].at[i]) for i in range(count)
    ]
    for copy in copies:
        copy.start()
    for copy in copies:
        copy.wait()


def finish(arrays):
    return pl.pallas_call(
        finish_kernel,
        out_shape=tuple(jax.ShapeDtypeStruct(a.shape, a.dtype) for a in arrays),
        in_specs=[pl.BlockSpec(memory_space=pl.ANY)] * len(arrays),
        out_specs=(pl.BlockSpec(memory_space=pltpu.VMEM),) * len(arrays),
        scratch_shapes=[pltpu.SemaphoreType.DMA((len(arrays),))],
        compiler_params=pltpu.CompilerParams(vmem_limit_bytes=VMEM_LIMIT),
    )(*arrays)


def fused_body(
    tokens_fwd, route_fwd, gate_fwd, grad_out, route_bwd, gate_bwd, saved_pre, w_up, w_down, basis_q
):
    n, n_sec = lax.axis_size("expert"), lax.axis_size("section")
    count, features = tokens_fwd.shape
    cap = count // (n // 2)
    slots, units = saved_pre.shape[2:]
    rank = basis_q.shape[1]
    bf, f32 = jnp.bfloat16, jnp.float32
    vmem = pl.BlockSpec(memory_space=pltpu.VMEM)
    hbm = pl.BlockSpec(memory_space=pltpu.HBM)
    wide = [pltpu.VMEM((slots, features), bf)]
    square = [pltpu.VMEM((rank, units), f32)]
    half = (rank, features // 2)
    results = pl.pallas_call(
        functools.partial(fused_kernel, (n, n_sec, cap)),
        out_shape=(
            jax.ShapeDtypeStruct((count, features), bf),
            jax.ShapeDtypeStruct((count, features), bf),
            jax.ShapeDtypeStruct((rank, units), f32),
            jax.ShapeDtypeStruct((rank, features), bf),
        ),
        in_specs=[hbm, vmem, vmem, hbm, vmem, vmem, hbm, hbm, hbm, hbm],
        out_specs=(vmem,) * 4,
        scratch_shapes=[
            pltpu.VMEM((count, features), bf),
            pltpu.VMEM((count, features), bf),
            pltpu.VMEM((slots, units), bf),
            pltpu.VMEM((features, units), bf),
            pltpu.VMEM((units, features), bf),
            pltpu.VMEM((rank, features), f32),
            pltpu.VMEM((count, features), bf),
            pltpu.VMEM((count, features), bf),
        ]
        + wide * 4
        + [pltpu.VMEM((n * cap, features), bf)] * 2
        + square * 6
        + [
            pltpu.VMEM((rank, features), f32),
            pltpu.VMEM(half, f32),
            pltpu.VMEM(half, f32),
            pltpu.VMEM(half, bf),
            pltpu.VMEM(half, bf),
            pltpu.VMEM((rank, features), bf),
            pltpu.VMEM((slots, units), bf),
            pltpu.VMEM((slots, units), f32),
            pltpu.VMEM((count, rank), f32),
            pltpu.VMEM((slots, rank), f32),
            pltpu.SemaphoreType.DMA((6,)),
        ]
        + [pltpu.SemaphoreType.DMA((n,))] * 10
        + [pltpu.SemaphoreType.DMA((1 + 4 * (rank // BLOCK),))] * 2,
        compiler_params=pltpu.CompilerParams(
            collective_id=0, has_side_effects=True, vmem_limit_bytes=VMEM_LIMIT
        ),
    )(
        tokens_fwd, route_fwd[None], gate_fwd[None], grad_out, route_bwd[None], gate_bwd[None],
        saved_pre[0, 0], w_up[0], w_down[0], basis_q.T,
    )
    expert_out, grad_in, left, right = finish(results)
    return (expert_out, grad_in, left.T[None], right.T[None, None])


def solution(mesh):
    def choose(*arguments):
        n = lax.axis_size("expert")
        capacity = arguments[0].shape[0] // (n // 2)
        rank = arguments[9].shape[1]
        whole_tiles = capacity % 16 == 0 and rank % BLOCK == 0
        whole_tiles = whole_tiles and arguments[0].shape[1] % 256 == 0
        pairs = lax.axis_size("dp") == 2 and lax.axis_size("section") % 2 == 0
        return (fused_body if whole_tiles and pairs else body)(*arguments)

    return jax.shard_map(
        choose,
        mesh=mesh,
        in_specs=(
            P(("section", "expert", "dp"), None),
            P(("section", "expert", "dp")),
            P(("section", "expert", "dp")),
            P(("section", "expert", "dp"), None),
            P(("section", "expert", "dp")),
            P(("section", "expert", "dp")),
            P("section", "dp", None, "expert"),
            P("section", None, "expert"),
            P("section", "expert", None),
            P(),
        ),
        out_specs=(
            P(("section", "expert", "dp"), None),
            P(("section", "expert", "dp"), None),
            P("section", "expert", None),
            P("section", "expert", None, None),
        ),
        check_vma=False,
    )
```
